512 devices in a mesh: cfg: 2 (over x_hi), uly: 8 (over y), blk: 32 (over z, x_lo, core).
Axes of the slice: x: 4 (x_hi: 2, x_lo: 2; x = x_hi * 2 + x_lo), y: 8, z: 8, core: 2. Of those that a mesh axis runs over, the one named last changes fastest.
Arguments:
- query_tokens: bfloat16 [2, 8192, 3072], P('cfg', ('uly', 'blk')), may hold values from -8 to 8
- key_tokens: bfloat16 [2, 4096, 3072], P('cfg', ('uly', 'blk')), may hold values from -8 to 8
- value_tokens: bfloat16 [2, 4096, 3072], P('cfg', ('uly', 'blk')), may hold values from -6 to 6
Outputs:
- guided: bfloat16 [8192, 24, 128], P(('uly', 'blk'), None, 'cfg')
The draws below stay inside these ranges and needn't reach their ends.
All inputs are finite; a program needn't handle non-finite values.
Results may differ from the reference program's by a relative error of at most 0.008.
Values may be sent and summed in bfloat16 or wider, within the bound.
A program may use at most 64 MiB of HBM per device.

```python
import math
import jax
import jax.numpy as jnp
from jax import lax

D = 3072
HEADS = 24
HD = 128
QTOKENS = 8192
KTOKENS = 4096


def draw_query_tokens(key, part):
    key = jax.random.fold_in(key, 5)
    base = jnp.clip(1.6 * jax.random.normal(key, (2, QTOKENS, D), jnp.float32), -8.0, 8.0)
    return base.astype(jnp.bfloat16)


def draw_key_tokens(key, part):
    key = jax.random.fold_in(key, 9)
    base = jnp.clip(1.6 * jax.random.normal(key, (2, KTOKENS, D), jnp.float32), -8.0, 8.0)
    return base.astype(jnp.bfloat16)


def shard_levels(stream_key, shape, cuts, least, high):
    factor_of = 1.0
    for axis_at, shards_of in cuts:
        heights = jax.random.uniform(jax.random.fold_in(jax.random.fold_in(stream_key, 6), axis_at), (shards_of,), jnp.float32, least / len(cuts), high / len(cuts))
        factor_of = factor_of * jnp.repeat(jnp.exp(heights), shape[axis_at] // shards_of).reshape((-1,) + (1,) * (len(shape) - 1 - axis_at))
    return factor_of


def bell_draw(stream_key, dims, scale, reach, cuts=(), dtype=jnp.bfloat16):
    values = jax.random.normal(stream_key, dims, jnp.float32) * scale
    if len(cuts) > 0:
        values = shard_levels(stream_key, dims, cuts, -0.22, 0.18) * values
    return jnp.clip(values, min=-reach, max=reach).astype(dtype)


def setup_inputs(seed: int = 0) -> dict:
    arg_keys = jax.random.split(jax.random.key(seed), 4)
    return {
        "query_tokens": draw_query_tokens(jax.random.fold_in(arg_keys[3], 71), 0),
        "key_tokens": draw_key_tokens(jax.random.fold_in(arg_keys[3], 71), 0),
        "value_tokens": bell_draw(arg_keys[2], (2, KTOKENS, D), 1.0, 6.0, ((0, 2), (1, 256))),
    }


GUIDE = 6.0

def attend_branch(queries, keys_in, values_in):
    scaling = 1.0 / math.sqrt(HD)
    keys_f32 = keys_in.astype(jnp.float32).reshape(KTOKENS, HEADS, HD)
    values_f32 = values_in.astype(jnp.float32).reshape(KTOKENS, HEADS, HD)
    q_rows = math.gcd(QTOKENS, 128)
    q_blocks = queries.reshape(QTOKENS // q_rows, q_rows, HEADS, HD)

    def one_block(q_block):
        logits = jnp.einsum('qhd,khd->qhk', q_block.astype(jnp.float32), keys_f32) * scaling
        row_max = lax.optimization_barrier(jnp.max(logits, axis=-1, keepdims=True))
        exp_terms = jnp.exp(logits - row_max)
        row_total = lax.optimization_barrier(jnp.sum(exp_terms, axis=-1))
        weights = lax.optimization_barrier(exp_terms.astype(jnp.bfloat16)).astype(jnp.float32)
        mixed = jnp.einsum('qhk,khd->qhd', weights, values_f32) / row_total[..., None]
        return mixed.astype(jnp.bfloat16)
    result = lax.map(one_block, q_blocks)
    return result.reshape(QTOKENS, HEADS, HD)

def reference(query_tokens, key_tokens, value_tokens):
    conditional = attend_branch(query_tokens[0], key_tokens[0], value_tokens[0]).astype(jnp.float32)
    unconditional = attend_branch(query_tokens[1], key_tokens[1], value_tokens[1]).astype(jnp.float32)
    return (unconditional + GUIDE * (conditional - unconditional)).astype(jnp.bfloat16)
```

```python
import functools
import math

import jax
import jax.numpy as jnp
from jax import lax
from jax.experimental import pallas as pl
from jax.experimental.pallas import tpu as pltpu
from jax.sharding import PartitionSpec as P

GUIDE = 6.0
HD = 128
HEADS = 24
RING = 8
LOG2E = math.log2(math.e)
SCALE = LOG2E / math.sqrt(HD)
MESH = pl.DeviceIdType.MESH
F32 = jnp.float32
BF16 = jnp.bfloat16


def kernel(
    q_in, k_in, v_in, out,
    kv, q, acc, top, o_send, o_got,
    kv_got, q_got, ring_got, core_got, out_got,
    a2a_sent, edge_sent, ring_sent, core_sent, out_sent,
):
    c = lax.axis_index("cfg")
    y = lax.axis_index("uly")
    blk = lax.axis_index("blk")
    z = lax.div(blk, 4)
    xl = lax.rem(lax.div(blk, 2), 2)
    core = lax.rem(blk, 2)

    def device(c_, y_, z_, xl_, core_):
        return (c_, y_, z_ * 4 + xl_ * 2 + core_)

    def place(t, a_, r_, xl_, c_=c):
        return device(c_, a_, r_, xl_, core) if t == 0 else device(c_, r_, a_, xl_, core)

    at = (y, z)
    along = (z, y)
    apart = [xl if t == 0 else 1 - xl for t in range(2)]
    odd = [lax.rem(at[t], 2) for t in range(2)]
    active = [jnp.logical_or(apart[t] == 0, odd[t] == 0) for t in range(2)]
    head = [12 * t + jnp.where(apart[t] == 0, at[t], 8 + lax.div(at[t], 2)) for t in range(2)]
    mate = device(c, y, z, xl, 1 - core)

    def turn(a, j):
        return lax.rem(a + j, RING)

    barrier = pltpu.get_barrier_semaphore()
    peers = [mate, device(1 - c, y, z, xl, core), device(c, y, z, 1 - xl, core)]
    for j in range(1, RING):
        for x_ in (xl, 1 - xl):
            peers.append(device(c, turn(y, j), z, x_, core))
            peers.append(device(c, y, turn(z, j), x_, core))
    for p in peers:
        pl.semaphore_signal(barrier, inc=1, device_id=p, device_id_type=MESH)
    pl.semaphore_wait(barrier, len(peers))

    def targets(t):
        a = at[t]
        result = []
        for j in range(RING):
            to = turn(a, j)
            slot = ((RING - j) % RING) * 2 + apart[t]
            result.append((to, t, 12 * t + to, slot, (apart[t] == 0) if j == 0 else None))
        pair = lax.div(a, 2)
        for j in range(4):
            to = 2 * lax.rem(pair + j, 4)
            slot = lax.rem(a - to + RING, RING) * 2 + (1 - apart[t])
            here = jnp.logical_and(apart[t] == 1, odd[t] == 0) if j == 0 else None
            result.append((to, 1 - t, 12 * t + 8 + lax.div(to, 2), slot, here))
        return result

    def columns(h):
        return pl.ds(pl.multiple_of(h * HD, HD), HD)

    def send_piece(src, dst, sent, got, target, here, where, edge):
        def remote(sem):
            pltpu.make_async_remote_copy(
                src_ref=src, dst_ref=dst, send_sem=sem, recv_sem=got,
                device_id=target, device_id_type=MESH,
            ).start()

        if here is None:
            remote(sent)
            return

        @pl.when(here)
        def _():
            pltpu.make_async_copy(src, dst, got).start()

        @pl.when(jnp.logical_not(here))
        def _():
            remote(edge)

    where = [targets(0), targets(1)]
    for i in range(12):
        for part, ref in enumerate((k_in, v_in)):
            for t in range(2):
                to, x_, h, slot, here = where[t][i]
                send_piece(
                    ref.at[0, :, columns(h)], kv.at[t, 0, 0, part, slot],
                    a2a_sent.at[t], kv_got.at[t, part], place(t, to, along[t], x_), here,
                    where, edge_sent.at[t, 0 if i == 0 else 1],
                )
    for i in range(12):
        for t in range(2):
            to, x_, h, slot, here = where[t][i]
            send_piece(
                q_in.at[0, :, columns(h)], q.at[t, slot],
                a2a_sent.at[t], q_got.at[t], place(t, to, along[t], x_), here,
                where, edge_sent.at[t, 0 if i == 0 else 1],
            )

    def await_bytes(ref, sem):
        pltpu.make_async_copy(ref, ref, sem).wait()

    def pass_on(t, r, part):
        piece = kv.at[t, r, 0, part]
        ahead = r in (0, 7, 6) or (r == 5 and part == 0)
        back = r in (0, 1, 2) or (r == 3 and part == 1)
        for go, step in ((ahead, 1), (back, 7)):
            if go:
                there = (r - step) % RING
                pltpu.make_async_remote_copy(
                    src_ref=piece, dst_ref=kv.at[t, there, 0, part],
                    send_sem=ring_sent.at[t], recv_sem=ring_got.at[t, there, part],
                    device_id=place(t, at[t], turn(along[t], step), xl),
                    device_id_type=MESH,
                ).start()
        pltpu.make_async_remote_copy(
            src_ref=piece, dst_ref=kv.at[t, r, 1, part],
            send_sem=core_sent.at[t], recv_sem=core_got.at[t, r, part],
            device_id=mate, device_id_type=MESH,
        ).start()

    def relay(t, *offsets):
        for r, part in [(r, part) for r in offsets for part in range(2)]:
            if r == 0:
                await_bytes(kv.at[t, 0, 0, part], kv_got.at[t, part])
            else:
                await_bytes(kv.at[t, r, 0, part], ring_got.at[t, r, part])
            pass_on(t, r, part)

    def attend(t, offsets, first):
        for r in offsets:
            for part in range(2):
                await_bytes(kv.at[t, r, 1, part], core_got.at[t, r, part])
        ones = jnp.ones((256, HD), BF16)
        for b in range(2):
            rows = q[t, 8 * b : 8 * b + 8].reshape(256, HD)
            span = pl.ds(256 * b, 256)
            logits = [
                lax.dot_general(
                    rows, kv[t, r, w, 0].reshape(256, HD), (((1,), (1,)), ((), ())),
                    preferred_element_type=F32,
                )
                for r in offsets
                for w in range(2)
            ]
            peak = logits[0]
            for s in logits[1:]:
                peak = jnp.maximum(peak, s)
            peak = jnp.max(peak, axis=1, keepdims=True) * SCALE
            if not first:
                before = top[t, span, 0:1]
                peak = jnp.maximum(before, peak)
            total = None
            for i, (r, w) in enumerate([(r, w) for r in offsets for w in range(2)]):
                weights = jnp.exp2(logits[i] * SCALE - peak).astype(BF16)
                values = jnp.concatenate([kv[t, r, w, 1].reshape(256, HD), ones], axis=1)
                term = jnp.dot(weights, values, preferred_element_type=F32)
                total = term if total is None else total + term
            if not first:
                total = total + acc[t, span] * jnp.exp2(before - peak)
            acc[t, span] = total
            top[t, span] = jnp.broadcast_to(peak, (256, HD))

    def both(f, *args):
        for t in range(2):
            pl.when(active[t])(functools.partial(f, t, *args))

    both(relay, 0)
    both(lambda t: await_bytes(q.at[t], q_got.at[t]))
    both(relay, 1, 7)
    both(attend, (0,), True)
    both(relay, 2, 6)
    both(attend, (1, 7), False)
    both(relay, 3, 5)
    both(attend, (2, 6), False)
    both(relay, 4)
    both(attend, (3, 5), False)

    def finish(t):
        attend(t, (4,), False)
        whole = acc[t]
        result = (whole[:, :HD] / whole[:, HD:]).reshape(16, 2, 16, HD)
        upper, lower = result[:, 0].reshape(256, HD), result[:, 1].reshape(256, HD)
        left = lax.broadcasted_iota(jnp.int32, (256, HD), 1) < 64
        o_send[t, 0] = jnp.where(left, upper, pltpu.roll(lower, 64, 1)).astype(BF16).reshape(16, 16, HD)
        o_send[t, 1] = jnp.where(left, pltpu.roll(upper, 64, 1), lower).astype(BF16).reshape(16, 16, HD)
        for j in range(RING):
            for b in range(2):
                for other in range(2):
                    c_ = c if other == 0 else 1 - c
                    x_ = xl if b == 0 else 1 - xl
                    src = o_send.at[t, c_, 2 * j + b]
                    dst = o_got.at[head[t], c]
                    if j == b == other == 0:
                        pltpu.make_async_copy(src, dst, out_got.at[0]).start()
                        continue
                    pltpu.make_async_remote_copy(
                        src_ref=src, dst_ref=dst,
                        send_sem=out_sent.at[t], recv_sem=out_got.at[0],
                        device_id=place(t, turn(at[t], j), along[t], x_, c_),
                        device_id_type=MESH,
                    ).start()

    both(finish)

    for t in range(2):
        await_bytes(kv.at[t, pl.ds(0, 5), 0, 0, pl.ds(0, 8)], a2a_sent.at[t])
        for e, (i, here) in enumerate(((0, where[t][0][4]), (8, where[t][8][4]))):
            @pl.when(jnp.logical_not(here))
            def _(t=t, e=e):
                await_bytes(kv.at[t, 0, 0, 0, pl.ds(0, 4)], edge_sent.at[t, e])

    def drain(t):
        await_bytes(kv.at[t, pl.ds(0, 7), 0], ring_sent.at[t])
        await_bytes(kv.at[t, :, 0], core_sent.at[t])
        await_bytes(kv.at[t, 0, 0, 0, pl.ds(0, 15)], out_sent.at[t])
        await_bytes(kv.at[t, 0, 0, 0], out_sent.at[t])

    await_bytes(o_got, out_got.at[0])
    conditional, unconditional = o_got[:, 0].astype(F32), o_got[:, 1].astype(F32)
    out[...] = (unconditional + GUIDE * (conditional - unconditional)).astype(BF16)
    both(drain)


def local(query_tokens, key_tokens, value_tokens):
    anywhere = pl.BlockSpec(memory_space=pl.ANY)
    dma = pltpu.SemaphoreType.DMA
    guided = pl.pallas_call(
        kernel,
        out_shape=jax.ShapeDtypeStruct((HEADS, 16, HD), BF16),
        in_specs=[anywhere] * 3,
        out_specs=pl.BlockSpec(memory_space=pltpu.VMEM),
        scratch_shapes=[
            pltpu.VMEM((2, RING, 2, 2, 16, 16, HD), BF16),
            pltpu.VMEM((2, 16, 32, HD), BF16),
            pltpu.VMEM((2, 512, 2 * HD), F32),
            pltpu.VMEM((2, 512, HD), F32),
            pltpu.VMEM((2, 2, 16, 16, HD), BF16),
            pltpu.VMEM((HEADS, 2, 16, HD), BF16),
            dma((2, 2)), dma((2,)), dma((2, RING, 2)), dma((2, RING, 2)), dma((1,)),
            dma((2,)), dma((2, 2)), dma((2,)), dma((2,)), dma((2,)),
        ],
        compiler_params=pltpu.CompilerParams(
            collective_id=0, has_side_effects=True, vmem_limit_bytes=48 << 20
        ),
        name="guided_attention",
    )(query_tokens, key_tokens, value_tokens)
    halves = guided.reshape(HEADS, 16, 2, HD // 2)
    return halves.transpose(2, 1, 0, 3).reshape(32, HEADS, HD // 2)


def solution(mesh):
    tokens = P("cfg", ("uly", "blk"), None)
    return jax.shard_map(
        local, mesh=mesh, in_specs=(tokens,) * 3,
        out_specs=P(("uly", "blk"), None, "cfg"), check_vma=False,
    )
```

```python
import functools
import math

import jax
import jax.numpy as jnp
from jax import lax
from jax.experimental import pallas as pl
from jax.experimental.pallas import tpu as pltpu
from jax.sharding import PartitionSpec as P

GUIDE = 6.0
FAR_FIRST = (4, 3, 5, 2, 6, 1, 7, 0)
SENDS = (4, 10, 3, 5, 9, 11, 2, 6, 8, 1, 7, 0)
HD = 128
HEADS = 24
RING = 8
LOG2E = math.log2(math.e)
SCALE = LOG2E / math.sqrt(HD)
MESH = pl.DeviceIdType.MESH
F32 = jnp.float32
BF16 = jnp.bfloat16


def kernel(
    q_in, k_in, v_in, out,
    kv_out, q_out, kv, q, acc, top, o_send, o_got, spread,
    staged,    kv_got, q_got, ring_got, core_got, out_got,
    a2a_sent, edge_sent, ring_sent, core_sent, out_sent,
):
    c = lax.axis_index("cfg")
    y = lax.axis_index("uly")
    blk = lax.axis_index("blk")
    z = lax.div(blk, 4)
    xl = lax.rem(lax.div(blk, 2), 2)
    core = lax.rem(blk, 2)

    def device(c_, y_, z_, xl_, core_):
        return (c_, y_, z_ * 4 + xl_ * 2 + core_)

    def place(t, a_, r_, xl_, c_=c):
        return device(c_, a_, r_, xl_, core) if t == 0 else device(c_, r_, a_, xl_, core)

    at = (y, z)
    along = (z, y)
    apart = [xl if t == 0 else 1 - xl for t in range(2)]
    odd = [lax.rem(at[t], 2) for t in range(2)]
    active = [jnp.logical_or(apart[t] == 0, odd[t] == 0) for t in range(2)]
    head = [12 * t + jnp.where(apart[t] == 0, at[t], 8 + lax.div(at[t], 2)) for t in range(2)]
    mate = device(c, y, z, xl, 1 - core)

    def turn(a, j):
        return lax.rem(a + j, RING)

    barrier = pltpu.get_barrier_semaphore()
    peers = [mate, device(1 - c, y, z, xl, core), device(c, y, z, 1 - xl, core)]
    for j in FAR_FIRST[:-1]:
        for x_ in (xl, 1 - xl):
            peers.append(device(c, turn(y, j), z, x_, core))
            peers.append(device(c, y, turn(z, j), x_, core))
    for p in peers:
        pl.semaphore_signal(barrier, inc=1, device_id=p, device_id_type=MESH)
    def columns(h):
        return pl.ds(h * HD, HD)

    for h in range(HEADS):
        for part, ref in enumerate((k_in, v_in)):
            pltpu.make_async_copy(ref.at[0, :, columns(h)], kv_out.at[h, part], staged.at[0]).start()
    for h in range(HEADS):
        pltpu.make_async_copy(q_in.at[0, :, columns(h)], q_out.at[h], staged.at[1]).start()

    def await_bytes(ref, sem):
        pltpu.make_async_copy(ref, ref, sem).wait()

    pl.semaphore_wait(barrier, len(peers))

    def targets(t):
        a = at[t]
        result = []
        for j in range(RING):
            to = turn(a, j)
            slot = ((RING - j) % RING) * 2 + apart[t]
            result.append((to, t, 12 * t + to, slot, (apart[t] == 0) if j == 0 else None))
        pair = lax.div(a, 2)
        for j in range(4):
            to = 2 * lax.rem(pair + j, 4)
            slot = lax.rem(a - to + RING, RING) * 2 + (1 - apart[t])
            here = jnp.logical_and(apart[t] == 1, odd[t] == 0) if j == 0 else None
            result.append((to, 1 - t, 12 * t + 8 + lax.div(to, 2), slot, here))
        return result

    def send_piece(src, dst, sent, got, target, here, edge):
        def remote(sem):
            pltpu.make_async_remote_copy(
                src_ref=src, dst_ref=dst, send_sem=sem, recv_sem=got,
                device_id=target, device_id_type=MESH,
            ).start()

        if here is None:
            remote(sent)
            return

        @pl.when(here)
        def _():
            pltpu.make_async_copy(src, dst, got).start()

        @pl.when(jnp.logical_not(here))
        def _():
            remote(edge)

    where = [targets(0), targets(1)]
    await_bytes(kv_out, staged.at[0])
    for i in SENDS:
        for t in range(2):
            to, x_, h, slot, here = where[t][i]
            send_piece(
                kv_out.at[h], kv.at[t, 0, 0, :, slot],
                a2a_sent.at[t], kv_got.at[t], place(t, to, along[t], x_), here,
                edge_sent.at[t, 0 if i == 0 else 1],
            )
    await_bytes(q_out, staged.at[1])
    for i in SENDS:
        for t in range(2):
            to, x_, h, slot, here = where[t][i]
            send_piece(
                q_out.at[h], q.at[t, slot],
                a2a_sent.at[t], q_got.at[t], place(t, to, along[t], x_), here,
                edge_sent.at[t, 0 if i == 0 else 1],
            )

    def pass_on(t, r, part):
        piece = kv.at[t, r, 0, part]
        ahead = r in (0, 7, 6) or (r == 5 and part == 0)
        back = r in (0, 1, 2) or (r == 3 and part == 1)
        for go, step in ((ahead, 1), (back, 7)):
            if go:
                there = (r - step) % RING
                pltpu.make_async_remote_copy(
                    src_ref=piece, dst_ref=kv.at[t, there, 0, part],
                    send_sem=ring_sent.at[t], recv_sem=ring_got.at[t, there, part],
                    device_id=place(t, at[t], turn(along[t], step), xl),
                    device_id_type=MESH,
                ).start()
        pltpu.make_async_remote_copy(
            src_ref=piece, dst_ref=kv.at[t, r, 1, part],
            send_sem=core_sent.at[t], recv_sem=core_got.at[t, r, part],
            device_id=mate, device_id_type=MESH,
        ).start()

    def relay(*offsets):
        for part in range(2):
            for t in range(2):
                @pl.when(active[t])
                def _(t=t, part=part):
                    for r in offsets:
                        if r != 0:
                            await_bytes(kv.at[t, r, 0, part], ring_got.at[t, r, part])
                        elif part == 0:
                            await_bytes(kv.at[t, 0, 0], kv_got.at[t])
                        pass_on(t, r, part)

    def attend(t, offsets, first):
        for r in offsets:
            for part in range(2):
                await_bytes(kv.at[t, r, 1, part], core_got.at[t, r, part])
        ones = jnp.ones((256, HD), BF16)
        chunks = [(r, w) for r in offsets for w in range(2)]

        def score(b):
            rows = q[t, 8 * b : 8 * b + 8].reshape(256, HD)
            return [
                lax.dot_general(
                    rows, kv[t, r, w, 0].reshape(256, HD), (((1,), (1,)), ((), ())),
                    preferred_element_type=F32,
                )
                for r, w in chunks
            ]

        def mix(b, logits):
            span = pl.ds(256 * b, 256)
            peak = functools.reduce(jnp.maximum, logits)
            peak = jnp.max(peak, axis=1, keepdims=True) * SCALE
            if not first:
                before = top[t, span, 0:1]
                peak = jnp.maximum(before, peak)
            weights = [jnp.exp2(s * SCALE - peak) for s in logits]
            total = None
            for p, (r, w) in zip(weights, chunks):
                values = jnp.concatenate([kv[t, r, w, 1].reshape(256, HD), ones], axis=1)
                term = jnp.dot(p.astype(BF16), values, preferred_element_type=F32)
                total = term if total is None else total + term
            if not first:
                total = total + acc[t, span] * jnp.exp2(before - peak)
            acc[t, span] = total
            top[t, span] = jnp.broadcast_to(peak, (256, HD))

        upper = score(0)
        lower = score(1)
        mix(0, upper)
        mix(1, lower)

    def both(f, *args):
        for t in range(2):
            pl.when(active[t])(functools.partial(f, t, *args))

    relay(0)
    both(lambda t: await_bytes(q.at[t], q_got.at[t]))
    relay(1, 7)
    both(attend, (0,), True)
    relay(2, 6)
    both(attend, (1, 7), False)
    relay(3, 5)
    both(attend, (2, 6), False)
    relay(4)
    both(attend, (3, 5), False)

    def finish(t):
        attend(t, (4,), False)
        whole = acc[t]
        result = (whole[:, :HD] / whole[:, HD:]).reshape(16, 2, 16, HD)
        upper, lower = result[:, 0].reshape(256, HD), result[:, 1].reshape(256, HD)
        left = lax.broadcasted_iota(jnp.int32, (256, HD), 1) < 64
        o_send[t, 0] = jnp.where(left, upper, pltpu.roll(lower, 64, 1)).astype(BF16).reshape(16, 16, HD)
        o_send[t, 1] = jnp.where(left, pltpu.roll(upper, 64, 1), lower).astype(BF16).reshape(16, 16, HD)
        for j in FAR_FIRST:
            for b in (1, 0):
                for other in (1, 0):
                    c_ = c if other == 0 else 1 - c
                    x_ = xl if b == 0 else 1 - xl
                    src = o_send.at[t, c_, 2 * j + b]
                    dst = o_got.at[head[t], c]
                    if j == b == other == 0:
                        pltpu.make_async_copy(src, dst, out_got.at[0]).start()
                        continue
                    pltpu.make_async_remote_copy(
                        src_ref=src, dst_ref=dst,
                        send_sem=out_sent.at[t], recv_sem=out_got.at[0],
                        device_id=place(t, turn(at[t], j), along[t], x_, c_),
                        device_id_type=MESH,
                    ).start()

    both(finish)

    for t in range(2):
        await_bytes(kv.at[t, pl.ds(0, 5), 0, 0, pl.ds(0, 8)], a2a_sent.at[t])
        for e, (i, here) in enumerate(((0, where[t][0][4]), (8, where[t][8][4]))):
            @pl.when(jnp.logical_not(here))
            def _(t=t, e=e):
                await_bytes(kv.at[t, 0, 0, 0, pl.ds(0, 4)], edge_sent.at[t, e])

    def drain(t):
        await_bytes(kv.at[t, pl.ds(0, 7), 0], ring_sent.at[t])
        await_bytes(kv.at[t, :, 0], core_sent.at[t])
        await_bytes(kv.at[t, 0, 0, 0, pl.ds(0, 15)], out_sent.at[t])
        await_bytes(kv.at[t, 0, 0, 0], out_sent.at[t])

    await_bytes(o_got, out_got.at[0])
    for h in range(HEADS):
        conditional, unconditional = o_got[h, 0].astype(F32), o_got[h, 1].astype(F32)
        guided = unconditional + GUIDE * (conditional - unconditional)
        spread[pl.ds(h, 16, stride=HEADS), :] = guided
        spread[pl.ds(16 * HEADS + h, 16, stride=HEADS), :] = pltpu.roll(guided, 64, 1)
    out[...] = spread[...].reshape(32, HEADS, HD)[:, :, : HD // 2].astype(BF16)
    both(drain)


def local(query_tokens, key_tokens, value_tokens):
    anywhere = pl.BlockSpec(memory_space=pltpu.HBM)
    dma = pltpu.SemaphoreType.DMA
    return pl.pallas_call(
        kernel,
        out_shape=jax.ShapeDtypeStruct((32, HEADS, HD // 2), BF16),
        in_specs=[anywhere] * 3,
        out_specs=pl.BlockSpec(memory_space=pltpu.VMEM),
        scratch_shapes=[
            pltpu.VMEM((HEADS, 2, 16, HD), BF16),
            pltpu.VMEM((HEADS, 32, HD), BF16),
            pltpu.VMEM((2, RING, 2, 2, 16, 16, HD), BF16),
            pltpu.VMEM((2, 16, 32, HD), BF16),
            pltpu.VMEM((2, 512, 2 * HD), F32),
            pltpu.VMEM((2, 512, HD), F32),
            pltpu.VMEM((2, 2, 16, 16, HD), BF16),
            pltpu.VMEM((HEADS, 2, 16, HD), BF16),
            pltpu.VMEM((32 * HEADS, HD), F32),
            dma((2,)), dma((2,)), dma((2,)), dma((2, RING, 2)), dma((2, RING, 2)), dma((1,)),
            dma((2,)), dma((2, 2)), dma((2,)), dma((2,)), dma((2,)),
        ],
        compiler_params=pltpu.CompilerParams(
            collective_id=0, has_side_effects=True, vmem_limit_bytes=64 * 2**20 - 2**16
        ),
        name="guided_attention",
    )(query_tokens, key_tokens, value_tokens)


def solution(mesh):
    tokens = P("cfg", ("uly", "blk"), None)
    return jax.shard_map(
        local, mesh=mesh, in_specs=(tokens,) * 3,
        out_specs=P(("uly", "blk"), None, "cfg"), check_vma=False,
    )
```

```python
import functools
import math

import jax
import jax.numpy as jnp
from jax import lax
from jax.experimental import pallas as pl
from jax.experimental.pallas import tpu as pltpu
from jax.sharding import PartitionSpec as P

GUIDE = 6.0
FAR_FIRST = (4, 3, 5, 2, 6, 1, 7, 0)
SENDS = (4, 10, 3, 5, 9, 11, 2, 6, 8, 1, 7, 0)
HD = 128
HEADS = 24
RING = 8
LOG2E = math.log2(math.e)
SCALE = LOG2E / math.sqrt(HD)
MESH = pl.DeviceIdType.MESH
F32 = jnp.float32
BF16 = jnp.bfloat16


def kernel(
    q_in, k_in, v_in, out,
    kv_out, q_out, kv, q, acc, top, o_send, o_got, spread,
    staged,    kv_got, q_got, ring_got, core_got, out_got,
    a2a_sent, edge_sent, ring_sent, core_sent, out_sent,
):
    c = lax.axis_index("cfg")
    y = lax.axis_index("uly")
    blk = lax.axis_index("blk")
    z = lax.div(blk, 4)
    xl = lax.rem(lax.div(blk, 2), 2)
    core = lax.rem(blk, 2)

    def device(c_, y_, z_, xl_, core_):
        return (c_, y_, z_ * 4 + xl_ * 2 + core_)

    def place(t, a_, r_, xl_, c_=c):
        return device(c_, a_, r_, xl_, core) if t == 0 else device(c_, r_, a_, xl_, core)

    at = (y, z)
    along = (z, y)
    apart = [xl if t == 0 else 1 - xl for t in range(2)]
    odd = [lax.rem(at[t], 2) for t in range(2)]
    active = [jnp.logical_or(apart[t] == 0, odd[t] == 1) for t in range(2)]
    head = [12 * t + jnp.where(apart[t] == 0, at[t], 8 + lax.div(at[t], 2)) for t in range(2)]
    mate = device(c, y, z, xl, 1 - core)

    def turn(a, j):
        return lax.rem(a + j, RING)

    barrier = pltpu.get_barrier_semaphore()
    peers = [mate, device(1 - c, y, z, xl, core), device(c, y, z, 1 - xl, core)]
    for j in FAR_FIRST[:-1]:
        for x_ in (xl, 1 - xl):
            peers.append(device(c, turn(y, j), z, x_, core))
            peers.append(device(c, y, turn(z, j), x_, core))
    for p in peers:
        pl.semaphore_signal(barrier, inc=1, device_id=p, device_id_type=MESH)
    def columns(h):
        return pl.ds(h * HD, HD)

    for h in range(HEADS):
        for part, ref in enumerate((k_in, v_in)):
            pltpu.make_async_copy(ref.at[0, :, columns(h)], kv_out.at[h, part], staged.at[0]).start()
    for h in range(HEADS):
        pltpu.make_async_copy(q_in.at[0, :, columns(h)], q_out.at[h], staged.at[1]).start()

    def await_bytes(ref, sem):
        pltpu.make_async_copy(ref, ref, sem).wait()

    pl.semaphore_wait(barrier, len(peers))

    def targets(t):
        a = at[t]
        result = []
        for j in range(RING):
            to = turn(a, j)
            slot = ((RING - j) % RING) * 2 + apart[t]
            result.append((to, t, 12 * t + to, slot, (apart[t] == 0) if j == 0 else None))
        pair = lax.div(a, 2)
        for j in range(4):
            to = 2 * lax.rem(pair + j, 4) + 1
            slot = lax.rem(a - to + RING, RING) * 2 + (1 - apart[t])
            here = jnp.logical_and(apart[t] == 1, odd[t] == 1) if j == 0 else None
            result.append((to, 1 - t, 12 * t + 8 + lax.div(to, 2), slot, here))
        return result

    def send_piece(src, dst, sent, got, target, here, edge):
        def remote(sem):
            pltpu.make_async_remote_copy(
                src_ref=src, dst_ref=dst, send_sem=sem, recv_sem=got,
                device_id=target, device_id_type=MESH,
            ).start()

        if here is None:
            remote(sent)
            return

        @pl.when(here)
        def _():
            pltpu.make_async_copy(src, dst, got).start()

        @pl.when(jnp.logical_not(here))
        def _():
            remote(edge)

    where = [targets(0), targets(1)]
    await_bytes(kv_out, staged.at[0])
    for i in SENDS:
        for t in range(2):
            to, x_, h, slot, here = where[t][i]
            send_piece(
                kv_out.at[h], kv.at[t, 0, 0, :, slot],
                a2a_sent.at[t], kv_got.at[t], place(t, to, along[t], x_), here,
                edge_sent.at[t, 0 if i == 0 else 1],
            )
    await_bytes(q_out, staged.at[1])
    for i in SENDS:
        for t in range(2):
            to, x_, h, slot, here = where[t][i]
            send_piece(
                q_out.at[h], q.at[t, slot],
                a2a_sent.at[t], q_got.at[t], place(t, to, along[t], x_), here,
                edge_sent.at[t, 0 if i == 0 else 1],
            )

    def pass_on(t, r, part):
        piece = kv.at[t, r, 0, part]
        ahead = r in (0, 7, 6) or (r == 5 and part == 0)
        back = r in (0, 1, 2) or (r == 3 and part == 1)
        for go, step in ((ahead, 1), (back, 7)):
            if go:
                there = (r - step) % RING
                pltpu.make_async_remote_copy(
                    src_ref=piece, dst_ref=kv.at[t, there, 0, part],
                    send_sem=ring_sent.at[t], recv_sem=ring_got.at[t, there, part],
                    device_id=place(t, at[t], turn(along[t], step), xl),
                    device_id_type=MESH,
                ).start()
        pltpu.make_async_remote_copy(
            src_ref=piece, dst_ref=kv.at[t, r, 1, part],
            send_sem=core_sent.at[t], recv_sem=core_got.at[t, r, part],
            device_id=mate, device_id_type=MESH,
        ).start()

    def relay(*offsets):
        for part in range(2):
            for t in range(2):
                @pl.when(active[t])
                def _(t=t, part=part):
                    for r in offsets:
                        if r != 0:
                            await_bytes(kv.at[t, r, 0, part], ring_got.at[t, r, part])
                        elif part == 0:
                            await_bytes(kv.at[t, 0, 0], kv_got.at[t])
                        pass_on(t, r, part)

    def attend(t, offsets, first):
        for r in offsets:
            for part in range(2):
                await_bytes(kv.at[t, r, 1, part], core_got.at[t, r, part])
        ones = jnp.ones((256, HD), BF16)
        chunks = [(r, w) for r in offsets for w in range(2)]

        def score(b):
            rows = q[t, 8 * b : 8 * b + 8].reshape(256, HD)
            return [
                lax.dot_general(
                    rows, kv[t, r, w, 0].reshape(256, HD), (((1,), (1,)), ((), ())),
                    preferred_element_type=F32,
                )
                for r, w in chunks
            ]

        def mix(b, logits):
            span = pl.ds(256 * b, 256)
            peak = functools.reduce(jnp.maximum, logits)
            peak = jnp.max(peak, axis=1, keepdims=True) * SCALE
            if not first:
                before = top[t, span, 0:1]
                peak = jnp.maximum(before, peak)
            weights = [jnp.exp2(s * SCALE - peak) for s in logits]
            total = None
            for p, (r, w) in zip(weights, chunks):
                values = jnp.concatenate([kv[t, r, w, 1].reshape(256, HD), ones], axis=1)
                term = jnp.dot(p.astype(BF16), values, preferred_element_type=F32)
                total = term if total is None else total + term
            if not first:
                total = total + acc[t, span] * jnp.exp2(before - peak)
            acc[t, span] = total
            top[t, span] = jnp.broadcast_to(peak, (256, HD))

        upper = score(0)
        lower = score(1)
        mix(0, upper)
        mix(1, lower)

    def both(f, *args):
        for t in range(2):
            pl.when(active[t])(functools.partial(f, t, *args))

    relay(0)
    both(lambda t: await_bytes(q.at[t], q_got.at[t]))
    both(attend, (0,), True)
    relay(1, 7)
    both(attend, (1, 7), False)
    relay(2, 6)
    both(attend, (2, 6), False)
    relay(3, 5)
    both(attend, (3, 5), False)
    relay(4)

    def finish(t):
        attend(t, (4,), False)
        whole = acc[t]
        result = (whole[:, :HD] / whole[:, HD:]).reshape(16, 2, 16, HD)
        upper, lower = result[:, 0].reshape(256, HD), result[:, 1].reshape(256, HD)
        left = lax.broadcasted_iota(jnp.int32, (256, HD), 1) < 64
        o_send[t, 0] = jnp.where(left, upper, pltpu.roll(lower, 64, 1)).astype(BF16).reshape(16, 16, HD)
        o_send[t, 1] = jnp.where(left, pltpu.roll(upper, 64, 1), lower).astype(BF16).reshape(16, 16, HD)
        for j in FAR_FIRST:
            for b in (1, 0):
                for other in (1, 0):
                    c_ = c if other == 0 else 1 - c
                    x_ = xl if b == 0 else 1 - xl
                    src = o_send.at[t, c_, 2 * j + b]
                    dst = o_got.at[head[t], c]
                    if j == b == other == 0:
                        pltpu.make_async_copy(src, dst, out_got.at[t]).start()
                        continue
                    pltpu.make_async_remote_copy(
                        src_ref=src, dst_ref=dst,
                        send_sem=out_sent.at[t], recv_sem=out_got.at[t],
                        device_id=place(t, turn(at[t], j), along[t], x_, c_),
                        device_id_type=MESH,
                    ).start()

    both(finish)

    for t in range(2):
        await_bytes(kv.at[t, pl.ds(0, 5), 0, 0, pl.ds(0, 8)], a2a_sent.at[t])
        for e, (i, here) in enumerate(((0, where[t][0][4]), (8, where[t][8][4]))):
            @pl.when(jnp.logical_not(here))
            def _(t=t, e=e):
                await_bytes(kv.at[t, 0, 0, 0, pl.ds(0, 4)], edge_sent.at[t, e])

    def drain(t):
        await_bytes(kv.at[t, pl.ds(0, 7), 0], ring_sent.at[t])
        await_bytes(kv.at[t, :, 0], core_sent.at[t])
        await_bytes(kv.at[t, 0, 0, 0, pl.ds(0, 15)], out_sent.at[t])
        await_bytes(kv.at[t, 0, 0, 0], out_sent.at[t])

    for h in range(HEADS):
        if h % 12 == 0:
            await_bytes(o_got.at[pl.ds(h, 12)], out_got.at[h // 12])
        conditional, unconditional = o_got[h, 0].astype(F32), o_got[h, 1].astype(F32)
        guided = unconditional + GUIDE * (conditional - unconditional)
        spread[pl.ds(h, 16, stride=HEADS), :] = guided
        spread[pl.ds(16 * HEADS + h, 16, stride=HEADS), :] = pltpu.roll(guided, 64, 1)
    out[...] = spread[...].reshape(32, HEADS, HD)[:, :, : HD // 2].astype(BF16)
    both(drain)


def local(query_tokens, key_tokens, value_tokens):
    inputs = [
        pltpu.with_memory_space_constraint(x, pltpu.HBM)
        for x in (query_tokens, key_tokens, value_tokens)
    ]
    anywhere = pl.BlockSpec(memory_space=pltpu.HBM)
    dma = pltpu.SemaphoreType.DMA
    return pl.pallas_call(
        kernel,
        out_shape=jax.ShapeDtypeStruct((32, HEADS, HD // 2), BF16),
        in_specs=[anywhere] * 3,
        out_specs=pl.BlockSpec(memory_space=pltpu.VMEM),
        scratch_shapes=[
            pltpu.VMEM((HEADS, 2, 16, HD), BF16),
            pltpu.VMEM((HEADS, 32, HD), BF16),
            pltpu.VMEM((2, RING, 2, 2, 16, 16, HD), BF16),
            pltpu.VMEM((2, 16, 32, HD), BF16),
            pltpu.VMEM((2, 512, 2 * HD), F32),
            pltpu.VMEM((2, 512, HD), F32),
            pltpu.VMEM((2, 2, 16, 16, HD), BF16),
            pltpu.VMEM((HEADS, 2, 16, HD), BF16),
            pltpu.VMEM((32 * HEADS, HD), F32),
            dma((2,)), dma((2,)), dma((2,)), dma((2, RING, 2)), dma((2, RING, 2)), dma((2,)),
            dma((2,)), dma((2, 2)), dma((2,)), dma((2,)), dma((2,)),
        ],
        compiler_params=pltpu.CompilerParams(
            collective_id=0, has_side_effects=True, vmem_limit_bytes=48 << 20
        ),
        name="guided_attention",
    )(*inputs)


def solution(mesh):
    tokens = P("cfg", ("uly", "blk"), None)
    return jax.shard_map(
        local, mesh=mesh, in_specs=(tokens,) * 3,
        out_specs=P(("uly", "blk"), None, "cfg"), check_vma=False,
    )
```

```python
import functools
import math

import jax
import jax.numpy as jnp
from jax import lax
from jax.experimental import pallas as pl
from jax.experimental.pallas import tpu as pltpu
from jax.sharding import PartitionSpec as P

GUIDE = 6.0
FAR_FIRST = (4, 3, 5, 2, 6, 1, 7, 0)
SENDS = (4, 10, 3, 5, 9, 11, 2, 6, 8, 1, 7, 0)
HD = 128
HEADS = 24
RING = 8
LOG2E = math.log2(math.e)
SCALE = LOG2E / math.sqrt(HD)
MESH = pl.DeviceIdType.MESH
F32 = jnp.float32
BF16 = jnp.bfloat16


def kernel(
    q_in, k_in, v_in, out,
    kv_out, q_out, kv, q, acc, top, o_send, o_got, spread,
    staged,    kv_got, q_got, ring_got, core_got, out_got,
    a2a_sent, edge_sent, ring_sent, core_sent, out_sent,
):
    c = lax.axis_index("cfg")
    y = lax.axis_index("uly")
    blk = lax.axis_index("blk")
    z = lax.div(blk, 4)
    xl = lax.rem(lax.div(blk, 2), 2)
    core = lax.rem(blk, 2)

    def device(c_, y_, z_, xl_, core_):
        return (c_, y_, z_ * 4 + xl_ * 2 + core_)

    def place(t, a_, r_, xl_, c_=c):
        return device(c_, a_, r_, xl_, core) if t == 0 else device(c_, r_, a_, xl_, core)

    at = (y, z)
    along = (z, y)
    apart = [xl if t == 0 else 1 - xl for t in range(2)]
    odd = [lax.rem(at[t], 2) for t in range(2)]
    active = [jnp.logical_or(apart[t] == 0, odd[t] == 1) for t in range(2)]
    head = [12 * t + jnp.where(apart[t] == 0, at[t], 8 + lax.div(at[t], 2)) for t in range(2)]
    mate = device(c, y, z, xl, 1 - core)

    def turn(a, j):
        return lax.rem(a + j, RING)

    barrier = pltpu.get_barrier_semaphore()
    peers = [mate, device(1 - c, y, z, xl, core), device(c, y, z, 1 - xl, core)]
    for j in FAR_FIRST[:-1]:
        for x_ in (xl, 1 - xl):
            peers.append(device(c, turn(y, j), z, x_, core))
            peers.append(device(c, y, turn(z, j), x_, core))
    for p in peers:
        pl.semaphore_signal(barrier, inc=1, device_id=p, device_id_type=MESH)
    def columns(h):
        return pl.ds(h * HD, HD)

    for h in range(HEADS):
        for part, ref in enumerate((k_in, v_in)):
            pltpu.make_async_copy(ref.at[0, :, columns(h)], kv_out.at[h, part], staged.at[0]).start()
    for h in range(HEADS):
        pltpu.make_async_copy(q_in.at[0, :, columns(h)], q_out.at[h], staged.at[1]).start()

    def await_bytes(ref, sem):
        pltpu.make_async_copy(ref, ref, sem).wait()

    pl.semaphore_wait(barrier, len(peers))

    def targets(t):
        a = at[t]
        result = []
        for j in range(RING):
            to = turn(a, j)
            slot = ((RING - j) % RING) * 2 + apart[t]
            result.append((to, t, 12 * t + to, slot, (apart[t] == 0) if j == 0 else None))
        pair = lax.div(a, 2)
        for j in range(4):
            to = 2 * lax.rem(pair + j, 4) + 1
            slot = lax.rem(a - to + RING, RING) * 2 + (1 - apart[t])
            here = jnp.logical_and(apart[t] == 1, odd[t] == 1) if j == 0 else None
            result.append((to, 1 - t, 12 * t + 8 + lax.div(to, 2), slot, here))
        return result

    def send_piece(src, dst, sent, got, target, here, edge):
        def remote(sem):
            pltpu.make_async_remote_copy(
                src_ref=src, dst_ref=dst, send_sem=sem, recv_sem=got,
                device_id=target, device_id_type=MESH,
            ).start()

        if here is None:
            remote(sent)
            return

        @pl.when(here)
        def _():
            pltpu.make_async_copy(src, dst, got).start()

        @pl.when(jnp.logical_not(here))
        def _():
            remote(edge)

    where = [targets(0), targets(1)]
    await_bytes(kv_out, staged.at[0])
    for i in SENDS:
        for t in range(2):
            to, x_, h, slot, here = where[t][i]
            send_piece(
                kv_out.at[h], kv.at[t, 0, 0, :, slot],
                a2a_sent.at[t], kv_got.at[t], place(t, to, along[t], x_), here,
                edge_sent.at[t, 0 if i == 0 else 1],
            )
    await_bytes(q_out, staged.at[1])
    for i in SENDS:
        for t in range(2):
            to, x_, h, slot, here = where[t][i]
            send_piece(
                q_out.at[h], q.at[t, slot],
                a2a_sent.at[t], q_got.at[t], place(t, to, along[t], x_), here,
                edge_sent.at[t, 0 if i == 0 else 1],
            )

    def pass_on(t, r, part):
        piece = kv.at[t, r, 0, part]
        ahead = r in (0, 7, 6) or (r == 5 and part == 0)
        back = r in (0, 1, 2) or (r == 3 and part == 1)
        for go, step in ((ahead, 1), (back, 7)):
            if go:
                there = (r - step) % RING
                pltpu.make_async_remote_copy(
                    src_ref=piece, dst_ref=kv.at[t, there, 0, part],
                    send_sem=ring_sent.at[t], recv_sem=ring_got.at[t, there, part],
                    device_id=place(t, at[t], turn(along[t], step), xl),
                    device_id_type=MESH,
                ).start()
        pltpu.make_async_remote_copy(
            src_ref=piece, dst_ref=kv.at[t, r, 1, part],
            send_sem=core_sent.at[t], recv_sem=core_got.at[t, r, part],
            device_id=mate, device_id_type=MESH,
        ).start()

    def relay(*offsets):
        for t in range(2):
            @pl.when(active[t])
            def _(t=t):
                for part in range(2):
                    for r in offsets:
                        if r != 0:
                            await_bytes(kv.at[t, r, 0, part], ring_got.at[t, r, part])
                        elif part == 0:
                            await_bytes(kv.at[t, 0, 0], kv_got.at[t])
                        pass_on(t, r, part)

    def attend(t, offsets, first, cores=(0, 1)):
        for r in offsets if 1 in cores else ():
            for part in range(2):
                await_bytes(kv.at[t, r, 1, part], core_got.at[t, r, part])
        ones = jnp.ones((256, HD), BF16)
        chunks = [(r, w) for r in offsets for w in cores]

        def score(b):
            rows = q[t, 8 * b : 8 * b + 8].reshape(256, HD)
            return [
                lax.dot_general(
                    rows, kv[t, r, w, 0].reshape(256, HD), (((1,), (1,)), ((), ())),
                    preferred_element_type=F32,
                )
                for r, w in chunks
            ]

        def mix(b, logits):
            span = pl.ds(256 * b, 256)
            peak = functools.reduce(jnp.maximum, logits)
            peak = jnp.max(peak, axis=1, keepdims=True) * SCALE
            if not first:
                before = top[t, span, 0:1]
                peak = jnp.maximum(before, peak)
            weights = [jnp.exp2(s * SCALE - peak) for s in logits]
            total = None
            for p, (r, w) in zip(weights, chunks):
                values = jnp.concatenate([kv[t, r, w, 1].reshape(256, HD), ones], axis=1)
                term = jnp.dot(p.astype(BF16), values, preferred_element_type=F32)
                total = term if total is None else total + term
            if not first:
                total = total + acc[t, span] * jnp.exp2(before - peak)
            acc[t, span] = total
            top[t, span] = jnp.broadcast_to(peak, (256, HD))

        upper = score(0)
        lower = score(1)
        mix(0, upper)
        mix(1, lower)

    def both(f, *args):
        for t in range(2):
            pl.when(active[t])(functools.partial(f, t, *args))

    relay(0)
    both(lambda t: await_bytes(q.at[t], q_got.at[t]))
    both(attend, (0,), True)
    relay(1, 7)
    both(attend, (1, 7), False)
    relay(2, 6)
    both(attend, (2, 6), False)
    relay(3, 5)
    both(attend, (3, 5), False)
    relay(4)
    both(attend, (4,), False, (0,))

    def finish(t):
        attend(t, (4,), False, (1,))
        whole = acc[t]
        result = (whole[:, :HD] / whole[:, HD:]).reshape(16, 2, 16, HD)
        upper, lower = result[:, 0].reshape(256, HD), result[:, 1].reshape(256, HD)
        left = lax.broadcasted_iota(jnp.int32, (256, HD), 1) < 64
        o_send[t, 0] = jnp.where(left, upper, pltpu.roll(lower, 64, 1)).astype(BF16).reshape(16, 16, HD)
        o_send[t, 1] = jnp.where(left, pltpu.roll(upper, 64, 1), lower).astype(BF16).reshape(16, 16, HD)
        for j in FAR_FIRST:
            for b in (1, 0):
                for other in (1, 0):
                    c_ = c if other == 0 else 1 - c
                    x_ = xl if b == 0 else 1 - xl
                    src = o_send.at[t, c_, 2 * j + b]
                    dst = o_got.at[head[t], c]
                    if j == b == other == 0:
                        pltpu.make_async_copy(src, dst, out_got.at[t]).start()
                        continue
                    pltpu.make_async_remote_copy(
                        src_ref=src, dst_ref=dst,
                        send_sem=out_sent.at[t], recv_sem=out_got.at[t],
                        device_id=place(t, turn(at[t], j), along[t], x_, c_),
                        device_id_type=MESH,
                    ).start()

    pl.when(jnp.logical_and(active[0], xl == 1))(functools.partial(finish, 0))
    pl.when(active[1])(functools.partial(finish, 1))
    pl.when(jnp.logical_and(active[0], xl == 0))(functools.partial(finish, 0))

    for t in range(2):
        await_bytes(kv.at[t, pl.ds(0, 5), 0, 0, pl.ds(0, 8)], a2a_sent.at[t])
        for e, (i, here) in enumerate(((0, where[t][0][4]), (8, where[t][8][4]))):
            @pl.when(jnp.logical_not(here))
            def _(t=t, e=e):
                await_bytes(kv.at[t, 0, 0, 0, pl.ds(0, 4)], edge_sent.at[t, e])

    def drain(t):
        await_bytes(kv.at[t, pl.ds(0, 7), 0], ring_sent.at[t])
        await_bytes(kv.at[t, :, 0], core_sent.at[t])

    def drain_out(t):
        await_bytes(kv.at[t, 0, 0, 0, pl.ds(0, 15)], out_sent.at[t])
        await_bytes(kv.at[t, 0, 0, 0], out_sent.at[t])

    both(drain)
    for h in range(HEADS):
        if h % 12 == 0:
            await_bytes(o_got.at[pl.ds(h, 12)], out_got.at[h // 12])
        conditional, unconditional = o_got[h, 0].astype(F32), o_got[h, 1].astype(F32)
        guided = unconditional + GUIDE * (conditional - unconditional)
        spread[pl.ds(h, 16, stride=HEADS), :] = guided
        spread[pl.ds(16 * HEADS + h, 16, stride=HEADS), :] = pltpu.roll(guided, 64, 1)
    out[...] = spread[...].reshape(32, HEADS, HD)[:, :, : HD // 2].astype(BF16)
    both(drain_out)


def local(query_tokens, key_tokens, value_tokens):
    inputs = [
        pltpu.with_memory_space_constraint(x, pltpu.HBM)
        for x in (query_tokens, key_tokens, value_tokens)
    ]
    anywhere = pl.BlockSpec(memory_space=pltpu.HBM)
    dma = pltpu.SemaphoreType.DMA
    return pl.pallas_call(
        kernel,
        out_shape=jax.ShapeDtypeStruct((32, HEADS, HD // 2), BF16),
        in_specs=[anywhere] * 3,
        out_specs=pl.BlockSpec(memory_space=pltpu.VMEM),
        scratch_shapes=[
            pltpu.VMEM((HEADS, 2, 16, HD), BF16),
            pltpu.VMEM((HEADS, 32, HD), BF16),
            pltpu.VMEM((2, RING, 2, 2, 16, 16, HD), BF16),
            pltpu.VMEM((2, 16, 32, HD), BF16),
            pltpu.VMEM((2, 512, 2 * HD), F32),
            pltpu.VMEM((2, 512, HD), F32),
            pltpu.VMEM((2, 2, 16, 16, HD), BF16),
            pltpu.VMEM((HEADS, 2, 16, HD), BF16),
            pltpu.VMEM((32 * HEADS, HD), F32),
            dma((2,)), dma((2,)), dma((2,)), dma((2, RING, 2)), dma((2, RING, 2)), dma((2,)),
            dma((2,)), dma((2, 2)), dma((2,)), dma((2,)), dma((2,)),
        ],
        compiler_params=pltpu.CompilerParams(
            collective_id=0, has_side_effects=True, vmem_limit_bytes=48 << 20
        ),
        name="guided_attention",
    )(*inputs)


def solution(mesh):
    tokens = P("cfg", ("uly", "blk"), None)
    return jax.shard_map(
        local, mesh=mesh, in_specs=(tokens,) * 3,
        out_specs=P(("uly", "blk"), None, "cfg"), check_vma=False,
    )
```

```python
import functools
import math

import jax
import jax.numpy as jnp
from jax import lax
from jax.experimental import pallas as pl
from jax.experimental.pallas import tpu as pltpu
from jax.sharding import PartitionSpec as P

GUIDE = 6.0
FAR_FIRST = (4, 3, 5, 2, 6, 1, 7, 0)
SENDS = (4, 10, 3, 5, 9, 11, 2, 6, 8, 1, 7, 0)
HD = 128
HEADS = 24
RING = 8
LOG2E = math.log2(math.e)
SCALE = LOG2E / math.sqrt(HD)
MESH = pl.DeviceIdType.MESH
F32 = jnp.float32
BF16 = jnp.bfloat16


def kernel(
    q_in, k_in, v_in, out,
    kv_out, q_out, kv, q, acc, top, o_send, o_got, spread,
    staged,    kv_got, q_got, ring_got, core_got, out_got,
    a2a_sent, edge_sent, ring_sent, core_sent, out_sent,
):
    c = lax.axis_index("cfg")
    y = lax.axis_index("uly")
    blk = lax.axis_index("blk")
    z = lax.div(blk, 4)
    xl = lax.rem(lax.div(blk, 2), 2)
    core = lax.rem(blk, 2)

    def device(c_, y_, z_, xl_, core_):
        return (c_, y_, z_ * 4 + xl_ * 2 + core_)

    def place(t, a_, r_, xl_, c_=c):
        return device(c_, a_, r_, xl_, core) if t == 0 else device(c_, r_, a_, xl_, core)

    at = (y, z)
    along = (z, y)
    apart = [xl if t == 0 else 1 - xl for t in range(2)]
    odd = [lax.rem(at[t], 2) for t in range(2)]
    active = [jnp.logical_or(apart[t] == 0, odd[t] == 1) for t in range(2)]
    head = [12 * t + jnp.where(apart[t] == 0, at[t], 8 + lax.div(at[t], 2)) for t in range(2)]
    mate = device(c, y, z, xl, 1 - core)

    def turn(a, j):
        return lax.rem(a + j, RING)

    barrier = pltpu.get_barrier_semaphore()
    peers = [mate, device(1 - c, y, z, xl, core), device(c, y, z, 1 - xl, core)]
    for j in FAR_FIRST[:-1]:
        for x_ in (xl, 1 - xl):
            peers.append(device(c, turn(y, j), z, x_, core))
            peers.append(device(c, y, turn(z, j), x_, core))
    for p in peers:
        pl.semaphore_signal(barrier, inc=1, device_id=p, device_id_type=MESH)
    def columns(h):
        return pl.ds(h * HD, HD)

    for h in range(HEADS):
        for part, ref in enumerate((k_in, v_in)):
            pltpu.make_async_copy(ref.at[0, :, columns(h)], kv_out.at[h, part], staged.at[0]).start()
    for h in range(HEADS):
        pltpu.make_async_copy(q_in.at[0, :, columns(h)], q_out.at[h], staged.at[1]).start()

    def await_bytes(ref, sem):
        pltpu.make_async_copy(ref, ref, sem).wait()

    pl.semaphore_wait(barrier, len(peers))

    def targets(t):
        a = at[t]
        result = []
        for j in range(RING):
            to = turn(a, j)
            slot = ((RING - j) % RING) * 2 + apart[t]
            result.append((to, t, 12 * t + to, slot, (apart[t] == 0) if j == 0 else None))
        pair = lax.div(a, 2)
        for j in range(4):
            to = 2 * lax.rem(pair + j, 4) + 1
            slot = lax.rem(a - to + RING, RING) * 2 + (1 - apart[t])
            here = jnp.logical_and(apart[t] == 1, odd[t] == 1) if j == 0 else None
            result.append((to, 1 - t, 12 * t + 8 + lax.div(to, 2), slot, here))
        return result

    def send_piece(src, dst, sent, got, target, here, edge):
        def remote(sem):
            pltpu.make_async_remote_copy(
                src_ref=src, dst_ref=dst, send_sem=sem, recv_sem=got,
                device_id=target, device_id_type=MESH,
            ).start()

        if here is None:
            remote(sent)
            return

        @pl.when(here)
        def _():
            pltpu.make_async_copy(src, dst, got).start()

        @pl.when(jnp.logical_not(here))
        def _():
            remote(edge)

    where = [targets(0), targets(1)]
    await_bytes(kv_out, staged.at[0])
    for i in SENDS:
        for t in range(2):
            to, x_, h, slot, here = where[t][i]
            send_piece(
                kv_out.at[h], kv.at[t, 0, 0, :, slot],
                a2a_sent.at[t], kv_got.at[t], place(t, to, along[t], x_), here,
                edge_sent.at[t, 0 if i == 0 else 1],
            )
    await_bytes(q_out, staged.at[1])
    for i in SENDS:
        for t in range(2):
            to, x_, h, slot, here = where[t][i]
            send_piece(
                q_out.at[h], q.at[t, slot],
                a2a_sent.at[t], q_got.at[t], place(t, to, along[t], x_), here,
                edge_sent.at[t, 0 if i == 0 else 1],
            )

    def pass_on(t, r, part):
        piece = kv.at[t, r, 0, part]
        ahead = r in (0, 7, 6) or (r == 5 and part == 0)
        back = r in (0, 1, 2) or (r == 3 and part == 1)
        for go, step in ((ahead, 1), (back, 7)):
            if go:
                there = (r - step) % RING
                pltpu.make_async_remote_copy(
                    src_ref=piece, dst_ref=kv.at[t, there, 0, part],
                    send_sem=ring_sent.at[t], recv_sem=ring_got.at[t, there, part],
                    device_id=place(t, at[t], turn(along[t], step), xl),
                    device_id_type=MESH,
                ).start()
        pltpu.make_async_remote_copy(
            src_ref=piece, dst_ref=kv.at[t, r, 1, part],
            send_sem=core_sent.at[t], recv_sem=core_got.at[t, r, part],
            device_id=mate, device_id_type=MESH,
        ).start()

    def relay(*offsets):
        for t in range(2):
            @pl.when(active[t])
            def _(t=t):
                for part in range(2):
                    for r in offsets:
                        if r != 0:
                            await_bytes(kv.at[t, r, 0, part], ring_got.at[t, r, part])
                        elif part == 0:
                            await_bytes(kv.at[t, 0, 0], kv_got.at[t])
                        pass_on(t, r, part)

    def attend(t, offsets, first, cores=(0, 1)):
        for r in offsets if 1 in cores else ():
            for part in range(2):
                await_bytes(kv.at[t, r, 1, part], core_got.at[t, r, part])
        ones = jnp.ones((256, HD), BF16)
        chunks = [(r, w) for r in offsets for w in cores]

        def score(b):
            rows = q[t, 8 * b : 8 * b + 8].reshape(256, HD)
            return [
                lax.dot_general(
                    rows, kv[t, r, w, 0].reshape(256, HD), (((1,), (1,)), ((), ())),
                    preferred_element_type=F32,
                )
                for r, w in chunks
            ]

        def mix(b, logits):
            span = pl.ds(256 * b, 256)
            peak = functools.reduce(jnp.maximum, logits)
            peak = jnp.max(peak, axis=1, keepdims=True) * SCALE
            if not first:
                before = top[t, span, 0:1]
                peak = jnp.maximum(before, peak)
            weights = [jnp.exp2(s * SCALE - peak) for s in logits]
            total = None
            for p, (r, w) in zip(weights, chunks):
                values = jnp.concatenate([kv[t, r, w, 1].reshape(256, HD), ones], axis=1)
                term = jnp.dot(p.astype(BF16), values, preferred_element_type=F32)
                total = term if total is None else total + term
            if not first:
                total = total + acc[t, span] * jnp.exp2(before - peak)
            acc[t, span] = total
            top[t, span] = jnp.broadcast_to(peak, (256, HD))

        upper = score(0)
        lower = score(1)
        mix(0, upper)
        mix(1, lower)

    def both(f, *args):
        for t in range(2):
            pl.when(active[t])(functools.partial(f, t, *args))

    relay(0)
    both(lambda t: await_bytes(q.at[t], q_got.at[t]))
    both(attend, (0,), True)
    relay(1, 7)
    both(attend, (1, 7), False, (0,))
    both(attend, (1, 7), False, (1,))
    relay(2, 6)
    both(attend, (2, 6), False, (0,))
    both(attend, (2, 6), False, (1,))
    relay(3, 5)
    both(attend, (3, 5), False, (0,))
    both(attend, (3, 5), False, (1,))
    relay(4)
    both(attend, (4,), False, (0,))

    def finish(t):
        attend(t, (4,), False, (1,))
        whole = acc[t]
        result = (whole[:, :HD] / whole[:, HD:]).reshape(16, 2, 16, HD)
        upper, lower = result[:, 0].reshape(256, HD), result[:, 1].reshape(256, HD)
        left = lax.broadcasted_iota(jnp.int32, (256, HD), 1) < 64
        o_send[t, 0] = jnp.where(left, upper, pltpu.roll(lower, 64, 1)).astype(BF16).reshape(16, 16, HD)
        o_send[t, 1] = jnp.where(left, pltpu.roll(upper, 64, 1), lower).astype(BF16).reshape(16, 16, HD)
        for j in FAR_FIRST:
            for b in (1, 0):
                for other in (1, 0):
                    c_ = c if other == 0 else 1 - c
                    x_ = xl if b == 0 else 1 - xl
                    src = o_send.at[t, c_, 2 * j + b]
                    dst = o_got.at[head[t], c]
                    if j == b == other == 0:
                        pltpu.make_async_copy(src, dst, out_got.at[t]).start()
                        continue
                    pltpu.make_async_remote_copy(
                        src_ref=src, dst_ref=dst,
                        send_sem=out_sent.at[t], recv_sem=out_got.at[t],
                        device_id=place(t, turn(at[t], j), along[t], x_, c_),
                        device_id_type=MESH,
                    ).start()

    pl.when(jnp.logical_and(active[0], xl == 1))(functools.partial(finish, 0))
    pl.when(active[1])(functools.partial(finish, 1))
    pl.when(jnp.logical_and(active[0], xl == 0))(functools.partial(finish, 0))

    for t in range(2):
        await_bytes(kv.at[t, pl.ds(0, 5), 0, 0, pl.ds(0, 8)], a2a_sent.at[t])
        for e, (i, here) in enumerate(((0, where[t][0][4]), (8, where[t][8][4]))):
            @pl.when(jnp.logical_not(here))
            def _(t=t, e=e):
                await_bytes(kv.at[t, 0, 0, 0, pl.ds(0, 4)], edge_sent.at[t, e])

    def drain(t):
        await_bytes(kv.at[t, pl.ds(0, 7), 0], ring_sent.at[t])
        await_bytes(kv.at[t, :, 0], core_sent.at[t])

    def drain_out(t):
        await_bytes(kv.at[t, 0, 0, 0, pl.ds(0, 15)], out_sent.at[t])
        await_bytes(kv.at[t, 0, 0, 0], out_sent.at[t])

    both(drain)
    for h in range(HEADS):
        if h % 12 == 0:
            await_bytes(o_got.at[pl.ds(h, 12)], out_got.at[h // 12])
        conditional, unconditional = o_got[h, 0].astype(F32), o_got[h, 1].astype(F32)
        guided = unconditional + GUIDE * (conditional - unconditional)
        spread[pl.ds(h, 16, stride=HEADS), :] = guided
        spread[pl.ds(16 * HEADS + h, 16, stride=HEADS), :] = pltpu.roll(guided, 64, 1)
    out[...] = spread[...].reshape(32, HEADS, HD)[:, :, : HD // 2].astype(BF16)
    both(drain_out)


def local(query_tokens, key_tokens, value_tokens):
    inputs = [
        pltpu.with_memory_space_constraint(x, pltpu.HBM)
        for x in (query_tokens, key_tokens, value_tokens)
    ]
    anywhere = pl.BlockSpec(memory_space=pltpu.HBM)
    dma = pltpu.SemaphoreType.DMA
    return pl.pallas_call(
        kernel,
        out_shape=jax.ShapeDtypeStruct((32, HEADS, HD // 2), BF16),
        in_specs=[anywhere] * 3,
        out_specs=pl.BlockSpec(memory_space=pltpu.VMEM),
        scratch_shapes=[
            pltpu.VMEM((HEADS, 2, 16, HD), BF16),
            pltpu.VMEM((HEADS, 32, HD), BF16),
            pltpu.VMEM((2, RING, 2, 2, 16, 16, HD), BF16),
            pltpu.VMEM((2, 16, 32, HD), BF16),
            pltpu.VMEM((2, 512, 2 * HD), F32),
            pltpu.VMEM((2, 512, HD), F32),
            pltpu.VMEM((2, 2, 16, 16, HD), BF16),
            pltpu.VMEM((HEADS, 2, 16, HD), BF16),
            pltpu.VMEM((32 * HEADS, HD), F32),
            dma((2,)), dma((2,)), dma((2,)), dma((2, RING, 2)), dma((2, RING, 2)), dma((2,)),
            dma((2,)), dma((2, 2)), dma((2,)), dma((2,)), dma((2,)),
        ],
        compiler_params=pltpu.CompilerParams(
            collective_id=0, has_side_effects=True, vmem_limit_bytes=48 << 20
        ),
        name="guided_attention",
    )(*inputs)


def solution(mesh):
    tokens = P("cfg", ("uly", "blk"), None)
    return jax.shard_map(
        local, mesh=mesh, in_specs=(tokens,) * 3,
        out_specs=P(("uly", "blk"), None, "cfg"), check_vma=False,
    )
```
